32 devices in a mesh: rep: 2 (over y), ep: 4 (over x, core), et: 4 (over z).
Axes of the slice: x: 2, y: 2, z: 4, core: 2. Of those that a mesh axis runs over, the one named last changes fastest.
Arguments:
- tokens: bfloat16 [1024, 3072], P(('rep', 'ep'), 'et'), parts along dimension 0, may hold values from -6 to 6
- out_grad: bfloat16 [1024, 3072], P(('rep', 'ep'), 'et'), parts along dimension 0, may hold values from -6 to 6
- route_ids: int32 [1024, 2], P(('rep', 'ep')), parts along dimension 0, may hold values from 0 to 3, all different within a row; in each aligned block of 128 rows (0 to 127, 128 to 255, ...) at most 72 rows name the same one
- route_weight: bfloat16 [1024, 2], P(('rep', 'ep')), parts along dimension 0, may hold values from 0.049804688 to 1
- w_gate: bfloat16 [3072, 32768], P(None, ('ep', 'et')), may hold values from -0.109375 to 0.109375
- w_up: bfloat16 [3072, 32768], P(None, ('ep', 'et')), may hold values from -0.109375 to 0.109375
- w_down: bfloat16 [32768, 3072], P(('ep', 'et')), may hold values from -0.0625 to 0.0625
Outputs:
- token_grad: bfloat16 [1024, 3072], P(('rep', 'ep'), 'et'), parts along dimension 0
- route_grad: float32 [1024, 2], P(('rep', 'ep')), parts along dimension 0
- gate_grad: bfloat16 [6144, 32768], P('rep', ('ep', 'et')), parts along dimension 0
- up_grad: bfloat16 [6144, 32768], P('rep', ('ep', 'et')), parts along dimension 0
- down_grad: bfloat16 [32768, 6144], P(('ep', 'et'), 'rep'), parts along dimension 1
The draws below stay inside these ranges and needn't reach their ends.
There are 2 independent parts, one for each index of `rep`. The reference program is written for one: setup_inputs(seed, part) draws one part's arguments, and reference() takes and returns one part's arrays. A program takes and returns all parts, laid end to end along the dimension named above; an argument that names none is the same for every part. Nothing has to cross between parts.
Inputs may be any that keep to these rules, and one draw needn't show every extreme that they name: `route_ids`: each token names 2 different experts. Among the 128 tokens of one index of ep, no expert is named by more than 72 tokens, and in some such block one expert is named by exactly 72.
All inputs are finite; a program needn't handle non-finite values.
Results may differ from the reference program's by a relative error of at most 0.012.
Values may be sent and summed in bfloat16 or wider, within the bound.
A program may use at most 192 MiB of HBM per device.

```python
import math
import jax
import jax.numpy as jnp
import numpy as np
from jax import lax

D = 3072
FF = 8192
EXP = 4
TOP = 2
TOK_DEV = 128
CAP = 72
TOKENS = 512
HID_DEV = 2048
N_EP = 4


def shard_levels(key, shape, cuts, low, high):
    factor_of = 1.0
    for dim, blocks in cuts:
        heights = jax.random.uniform(jax.random.fold_in(jax.random.fold_in(key, 6), dim), (blocks,), jnp.float32, low / len(cuts), high / len(cuts))
        factor_of = factor_of * jnp.repeat(jnp.exp(heights), shape[dim] // blocks).reshape((-1,) + (1,) * (len(shape) - 1 - dim))
    return factor_of


def assign_block(stream_key, own, number, rows, number_of, top, limit, skew):
    ranking = jax.random.permutation(stream_key, number_of)
    crowded, ordinary = shares(number_of, rows * top, limit, skew, True), shares(number_of, rows * top, limit, skew, False)
    places = jnp.arange(number_of)

    def named(lengths, rotation):
        used = int((lengths > 0).sum())
        fixed = max(1, used // 4)
        passed = fixed + (places - fixed + rotation * (used - fixed)) % max(1, number_of - fixed)
        return jnp.zeros((number_of,), jnp.int32).at[ranking[jnp.where(places < fixed, places, passed)]].set(jnp.asarray(lengths, jnp.int32))

    lengths = jnp.where(number % 4 == 0, named(crowded, number // 4), named(ordinary, number - number // 4 - 1))
    mixed = jax.random.permutation(jax.random.fold_in(own, 3), number_of)
    giver, taker = mixed[0:number_of // 2 * 2:2], mixed[1:number_of // 2 * 2:2]
    room = jnp.minimum(lengths[giver] - 1, limit - lengths[taker]) // 2
    room = jnp.where((giver == ranking[0]) | (taker == ranking[0]) | (lengths[taker] == 0), 0, jnp.maximum(room, 0))
    passed = jax.random.randint(jax.random.fold_in(own, 4), (number_of // 2,), 0, 1 << 20) % (room + 1)
    lengths = lengths.at[giver].add(-passed).at[taker].add(passed)
    items = jnp.searchsorted(jnp.cumsum(lengths), jnp.arange(rows * top), side="right").astype(jnp.int32)
    grid = items.reshape(top, rows).T
    grid = grid[jax.random.permutation(jax.random.fold_in(own, 1), rows)]
    rotation = jax.random.randint(jax.random.fold_in(own, 2), (rows, 1), 0, top)
    return jnp.take_along_axis(grid, (jnp.arange(top)[None, :] + rotation) % top, axis=1)


def shares(amount, total, bound, skew, full):
    loads = [(1 << 20) // math.isqrt(grade ** skew) + 1 for grade in range(1, amount + 1)]
    largest = bound if full else min(bound, max(-(-total // amount), total * loads[0] // sum(loads)))
    least = 1 if total - largest >= amount - 1 else 0
    holding, surplus = [largest] + [least] * (amount - 1), total - largest - least * (amount - 1)
    while surplus > 0:
        movable = [i for i in range(1, amount) if holding[i] < largest] or [i for i in range(1, amount) if holding[i] < bound]
        mass, left = sum([loads[i] for i in movable]), surplus
        for i in movable:
            more = min(bound - holding[i], max(1, left * loads[i] // mass), surplus)
            holding[i] = holding[i] + more
            surplus = surplus - more
    return np.array(holding)


def normal_values(own_key, shape, deviation, most, shards=(), dtype=jnp.bfloat16):
    level = shard_levels(own_key, shape, shards, -0.22, 0.18) if shards else 1.0
    result = jax.random.normal(own_key, shape, jnp.float32) * deviation * level
    return jnp.minimum(jnp.maximum(result, -most), most).astype(dtype)


def setup_inputs(seed: int = 0, part: int = 0) -> dict:
    seeds = jax.random.split(jax.random.key(seed), 8)
    part_keys = jax.random.split(jax.random.fold_in(seeds[7], part), 8)
    tokens = normal_values(part_keys[0], (TOKENS, D), 1.0, 6.0, ((0, 4), (1, 4)))
    out_grad = normal_values(part_keys[1], (TOKENS, D), 1.0, 6.0, ((0, 4), (1, 4)))
    route_ids_keys = jax.random.split(jax.random.fold_in(part_keys[2], 1), TOKENS // TOK_DEV)
    route_ids_turns = jax.random.permutation(jax.random.fold_in(part_keys[2], 3), TOKENS // TOK_DEV)
    route_ids = jax.vmap(lambda own, number: assign_block(jax.random.fold_in(part_keys[2], 2), own, number, TOK_DEV, EXP, TOP, CAP, 1))(route_ids_keys, route_ids_turns).reshape((TOKENS, TOP))
    route_weight = jnp.clip(jnp.exp(math.log(1.0) - 2.9996462 * jax.random.uniform(part_keys[3], (TOKENS, TOP), jnp.float32) ** shard_levels(part_keys[3], (TOKENS, TOP), ((0, 4),), -0.2, 0.2)), 0.049804688, 1.0).astype(jnp.bfloat16)
    w_gate = normal_values(seeds[4], (D, EXP * FF), D ** -0.5, 0.109375, ((1, 16),))
    w_up = normal_values(seeds[5], (D, EXP * FF), D ** -0.5, 0.109375, ((1, 16),))
    w_down = normal_values(seeds[6], (EXP * FF, D), FF ** -0.5, 0.0625, ((0, 16),))
    return {"tokens": tokens, "out_grad": out_grad, "route_ids": route_ids, "route_weight": route_weight, "w_gate": w_gate, "w_up": w_up, "w_down": w_down}


def reference(tokens, out_grad, route_ids, route_weight, w_gate, w_up, w_down):
    capacity = N_EP * CAP
    pieces = FF // HID_DEV
    token_grad = jnp.zeros((TOKENS, D), jnp.float32)
    route_grad = jnp.zeros((TOKENS, TOP), jnp.float32)
    gate_parts = []
    up_parts = []
    down_parts = []
    contract_rows = (((0,), (0,)), ((), ()))
    contract_hidden = (((1,), (1,)), ((), ()))
    for expert in range(EXP):
        expert_hit = route_ids == expert
        chosen = jnp.any(expert_hit, axis=1)
        index = jnp.nonzero(chosen, size=capacity, fill_value=0)[0].astype(jnp.int32)
        valid = (jnp.arange(capacity) < jnp.sum(chosen.astype(jnp.int32))).astype(jnp.float32)
        token_weight = jnp.sum(jnp.where(expert_hit, route_weight.astype(jnp.float32), 0.0), axis=1)
        scale = (token_weight[index] * valid)[:, None]
        rows_x = tokens[index]
        rows_dy = out_grad[index]
        first = expert * FF
        gate_cols = w_gate[:, first:first + FF]
        up_cols = w_up[:, first:first + FF]
        down_rows = w_down[first:first + FF, :]
        gate = jnp.dot(rows_x, gate_cols, preferred_element_type=jnp.float32)
        upper = jnp.dot(rows_x, up_cols, preferred_element_type=jnp.float32)
        sigma = jax.nn.sigmoid(gate)
        silu_gate = gate * sigma
        active = silu_gate * upper
        scaled = (scale * active).astype(jnp.bfloat16)
        raw_grad = lax.dot_general(rows_dy, down_rows, contract_hidden, preferred_element_type=jnp.float32)
        block_route = jnp.sum((active * raw_grad).reshape(capacity, pieces, HID_DEV), axis=2)
        slot_route = jnp.sum(block_route.astype(jnp.bfloat16).astype(jnp.float32), axis=1)
        hidden_grad = scale * raw_grad
        gate_delta = (hidden_grad * upper * sigma * (1.0 + gate * (1.0 - sigma))).astype(jnp.bfloat16)
        up_delta = (hidden_grad * silu_gate).astype(jnp.bfloat16)
        gate_parts.append(lax.dot_general(rows_x, gate_delta, contract_rows, preferred_element_type=jnp.float32).astype(jnp.bfloat16))
        up_parts.append(lax.dot_general(rows_x, up_delta, contract_rows, preferred_element_type=jnp.float32).astype(jnp.bfloat16))
        down_parts.append(lax.dot_general(scaled, rows_dy, contract_rows, preferred_element_type=jnp.float32).astype(jnp.bfloat16))
        slot_input = jnp.zeros((capacity, D), jnp.float32)
        for piece in range(pieces):
            lower = piece * HID_DEV
            upper_end = lower + HID_DEV
            block = lax.dot_general(gate_delta[:, lower:upper_end], gate_cols[:, lower:upper_end], contract_hidden,
                                    preferred_element_type=jnp.float32)
            block = block + lax.dot_general(up_delta[:, lower:upper_end], up_cols[:, lower:upper_end], contract_hidden,
                                            preferred_element_type=jnp.float32)
            slot_input = slot_input + block.astype(jnp.bfloat16).astype(jnp.float32)
        token_grad = token_grad.at[index].add(slot_input)
        token_route = jnp.zeros((TOKENS,), jnp.float32).at[index].add(slot_route * valid)
        route_grad = route_grad + jnp.where(expert_hit, token_route[:, None], 0.0)
    return (token_grad.astype(jnp.bfloat16), route_grad, jnp.concatenate(gate_parts, axis=1),
            jnp.concatenate(up_parts, axis=1), jnp.concatenate(down_parts, axis=0))
```

```python
import functools

import jax
import jax.numpy as jnp
from jax import lax
from jax.experimental import pallas as pl
from jax.experimental.pallas import tpu as pltpu
from jax.sharding import PartitionSpec as P

EXP = 4
CAP = 72
MESH = pl.DeviceIdType.MESH
VMEM_LIMIT = 60 * 1024 * 1024


def remote(src, dst, send_sem, recv_sem, device):
    return pltpu.make_async_remote_copy(
        src_ref=src,
        dst_ref=dst,
        send_sem=send_sem,
        recv_sem=recv_sem,
        device_id=device,
        device_id_type=MESH,
    )


def dispatch_kernel(
    n_ep, n_et, tok_ref, dy_ref, ids_ref, w_ref, x_ref, d_ref, sel_ref, scale_ref,
    rows, meta, recv_sem, z_sem, x_sem, s_sem, meta_send, meta_recv,
):
    group = n_ep // EXP
    chips = n_ep // 2
    me, i = lax.axis_index("ep"), lax.axis_index("et")
    chip, core = lax.div(me, 2), lax.rem(me, 2)
    sibling = chip * 2 + 1 - core
    own = (tok_ref, dy_ref)
    width = tok_ref.shape[1]
    count = tok_ref.shape[0]

    barrier = pltpu.get_barrier_semaphore()
    for k in range(1, n_ep):
        pl.semaphore_signal(
            barrier, inc=1, device_id={"ep": lax.rem(me + k, n_ep)}, device_id_type=MESH
        )

    @pl.when(i > 0)
    def _():
        pl.semaphore_signal(barrier, inc=1, device_id={"et": i - 1}, device_id_type=MESH)

    @pl.when(i < n_et - 1)
    def _():
        pl.semaphore_signal(barrier, inc=1, device_id={"et": i + 1}, device_id_type=MESH)

    ids = ids_ref[...]
    weight = w_ref[...]
    experts = lax.broadcasted_iota(jnp.int32, (8, count), 0)
    first, second = ids[0:1, :] == experts, ids[1:2, :] == experts
    hit = jnp.logical_or(first, second)
    earlier = lax.broadcasted_iota(jnp.int32, (count, count), 0) < lax.broadcasted_iota(
        jnp.int32, (count, count), 1
    )
    before = jnp.dot(
        jnp.where(hit, 1.0, 0.0).astype(jnp.bfloat16),
        jnp.where(earlier, 1.0, 0.0).astype(jnp.bfloat16),
        preferred_element_type=jnp.float32,
    )
    meta[me, 0:8, :] = jnp.where(hit, before, -1e6)
    meta[me, 8:16, :] = jnp.where(first, weight[0:1, :], 0.0) + jnp.where(
        second, weight[1:2, :], 0.0
    )

    neighbours = jnp.where(i > 0, 1, 0) + jnp.where(i < n_et - 1, 1, 0)
    pl.semaphore_wait(barrier, n_ep - 1 + neighbours)

    def block(a, p, j):
        return rows.at[a, p, j]

    def z_copy(a, j, way, src):
        return remote(
            src, block(a, me, j), z_sem.at[a, way, j], recv_sem.at[a, me, j],
            {"et": i + 1 if way == 0 else i - 1},
        )

    def x_copy(a, k, j, src):
        peer = lax.rem(chip + k, chips) * 2 + core
        return remote(
            src, block(a, me, j), x_sem.at[a, k, j], recv_sem.at[a, me, j], {"ep": peer}
        )

    def s_copy(a, p, j, src):
        return remote(
            src, block(a, p, j), s_sem.at[a, p, j], recv_sem.at[a, p, j], {"ep": sibling}
        )

    def meta_copy(k):
        return remote(
            meta.at[me], meta.at[me], meta_send.at[k], meta_recv.at[me],
            {"ep": lax.rem(me + k, n_ep)},
        )

    def arrive(a, p, j):
        remote(
            block(a, p, j), block(a, p, j), s_sem.at[a, p, j], recv_sem.at[a, p, j],
            {"ep": sibling},
        ).wait_recv()

    def fan(a, j, src):
        for k in range(1, chips):
            x_copy(a, k, j, src).start()
        s_copy(a, me, j, src).start()

    for k in range(1, n_ep):
        meta_copy(k).start()
    for a in range(2):
        @pl.when(i < n_et - 1)
        def _():
            z_copy(a, i, 0, own[a]).start()

        @pl.when(i > 0)
        def _():
            z_copy(a, i, 1, own[a]).start()

        fan(a, i, own[a])
    for a in range(2):
        rows[a, me, i] = own[a][...]

    def on_steps(s, act):
        @pl.when(i >= s)
        def _():
            act(i - s, 0)

        if s > 0:
            @pl.when(i + s < n_et)
            def _():
                act(i + s, 1)

    def from_chips(s):
        for a in range(2):
            def act(j, way):
                for k in range(1, chips):
                    p = lax.rem(chip + k, chips) * 2 + core
                    arrive(a, p, j)
                    s_copy(a, p, j, block(a, p, j)).start()

            on_steps(s, act)

    for s in range(1, n_et):
        for a in range(2):
            def act(j, way):
                arrive(a, me, j)
                if way == 0:
                    @pl.when(i < n_et - 1)
                    def _():
                        z_copy(a, j, 0, block(a, me, j)).start()
                else:
                    @pl.when(i > 0)
                    def _():
                        z_copy(a, j, 1, block(a, me, j)).start()

                fan(a, j, block(a, me, j))

            on_steps(s, act)
        from_chips(s - 1)
    from_chips(n_et - 1)

    for k in range(1, n_ep):
        p = lax.rem(me + k, n_ep)
        remote(
            meta.at[p], meta.at[p], meta_send.at[k], meta_recv.at[p], {"ep": p}
        ).wait_recv()
    expert = lax.div(me, group)
    slots = n_ep * CAP
    slot_row = lax.broadcasted_iota(jnp.int32, (slots, count), 0).astype(jnp.float32)
    scale = jnp.zeros((slots, 1), jnp.float32)
    for p in range(n_ep):
        place = meta[p, pl.ds(expert, 1), :]
        token_weight = meta[p, pl.ds(expert + 8, 1), :]
        match = slot_row == place + float(p * CAP)
        sel_ref[:, p * count : (p + 1) * count] = jnp.where(match, 1.0, 0.0).astype(jnp.bfloat16)
        scale = scale + jnp.sum(jnp.where(match, token_weight, 0.0), axis=1, keepdims=True)
    scale_ref[...] = jnp.broadcast_to(scale, scale_ref.shape)

    for a, out in ((0, x_ref), (1, d_ref)):
        for q in range(chips):
            for j in range(n_et):
                arrive(a, q * 2 + 1 - core, j)

        @pl.loop(0, n_et)
        def _(j):
            source = rows[a, :, j].reshape(n_ep * count, width)
            out[:, pl.ds(pl.multiple_of(j * width, width), width)] = jnp.dot(
                sel_ref[...], source, preferred_element_type=jnp.float32
            ).astype(jnp.bfloat16)

    for k in range(1, n_ep):
        meta_copy(k).wait_send()
    for a in range(2):
        for j in range(n_et):
            for k in range(1, chips):
                x_copy(a, k, j, block(a, me, j)).wait_send()
            for q in range(chips):
                p = q * 2 + core
                s_copy(a, p, j, block(a, p, j)).wait_send()

            @pl.when(jnp.logical_and(i < n_et - 1, i >= j))
            def _():
                z_copy(a, j, 0, block(a, me, j)).wait_send()

            @pl.when(jnp.logical_and(i > 0, i <= j))
            def _():
                z_copy(a, j, 1, block(a, me, j)).wait_send()


def combine_kernel(
    n_ep, n_et, gd_ref, ud_ref, wg_ref, wu_ref, place_ref, route_ref, ids_ref, tok_ref, rg_ref,
    wg, wu, part, sib_in, total, x_in, z_out, z_in, r_out, r_in, rz_out, rz_in,
    w_sem, s_send, s_recv, x_send, x_recv, z_send, z_recv, r_send, r_recv, rz_send, rz_recv,
):
    group = n_ep // EXP
    chips = n_ep // 2
    me, i = lax.axis_index("ep"), lax.axis_index("et")
    chip, core = lax.div(me, 2), lax.rem(me, 2)
    sibling = chip * 2 + 1 - core
    count, width = tok_ref.shape
    barrier = pltpu.get_barrier_semaphore()
    for k in range(1, n_ep):
        pl.semaphore_signal(
            barrier, inc=1, device_id={"ep": lax.rem(me + k, n_ep)}, device_id_type=MESH
        )
    for k in range(1, n_et):
        pl.semaphore_signal(
            barrier, inc=1, device_id={"et": lax.rem(i + k, n_et)}, device_id_type=MESH
        )

    def owner(s):
        return lax.rem(i + 1 + s, n_et)

    def weights(s):
        at = pl.ds(pl.multiple_of(owner(s) * width, width), width)
        return (
            pltpu.make_async_copy(wg_ref.at[at, :], wg.at[s], w_sem.at[0, s]),
            pltpu.make_async_copy(wu_ref.at[at, :], wu.at[s], w_sem.at[1, s]),
        )

    for s in range(n_et):
        for copy in weights(s):
            copy.start()
    transposed = (((1,), (1,)), ((), ()))
    routes = lax.dot_general(
        route_ref[...], place_ref[...], transposed, preferred_element_type=jnp.float32
    )
    for p in range(n_ep):
        r_out[p] = routes[:, p * count : (p + 1) * count]
    pl.semaphore_wait(barrier, n_ep - 1 + n_et - 1)

    def r_copy(k):
        p = lax.rem(me + k, n_ep)
        return remote(r_out.at[p], r_in.at[me], r_send.at[k], r_recv.at[me], {"ep": p})

    def rz_copy(k):
        return remote(
            rz_out, rz_in.at[i], rz_send.at[k], rz_recv.at[i], {"et": lax.rem(i + k, n_et)}
        )

    def s_copy(s, q):
        return remote(
            part.at[s, q * 2 + 1 - core], sib_in.at[s, q], s_send.at[s, q], s_recv.at[s, q],
            {"ep": sibling},
        )

    def x_copy(s, k):
        q = lax.rem(chip + k, chips)
        return remote(
            total.at[s, q], x_in.at[s, chip], x_send.at[s, k], x_recv.at[s, chip],
            {"ep": q * 2 + core},
        )

    def z_copy(s):
        return remote(
            z_out.at[s], z_in.at[i], z_send.at[s], z_recv.at[i], {"et": owner(s)}
        )

    for k in range(1, n_ep):
        r_copy(k).start()
    r_in[me] = r_out[me]

    def to_chips(s):
        for q in range(chips):
            s_copy(s, q).wait_recv()
            total[s, q] = (
                part[s, q * 2 + core].astype(jnp.float32) + sib_in[s, q].astype(jnp.float32)
            ).astype(jnp.bfloat16)
        for k in range(1, chips):
            x_copy(s, k).start()

    def step(s):
        for copy in weights(s):
            copy.wait()
        piece = lax.dot_general(
            gd_ref[...], wg[s], transposed, preferred_element_type=jnp.float32
        ) + lax.dot_general(ud_ref[...], wu[s], transposed, preferred_element_type=jnp.float32)
        placed = jnp.dot(
            place_ref[...], piece.astype(jnp.bfloat16), preferred_element_type=jnp.float32
        ).astype(jnp.bfloat16)
        part[s] = placed.reshape(n_ep, count, width)
        for q in range(chips):
            s_copy(s, q).start()

    step(0)

    @pl.loop(1, n_et)
    def _(s):
        step(s)
        to_chips(s - 1)

    to_chips(n_et - 1)

    for k in range(1, n_ep):
        p = lax.rem(me + k, n_ep)
        remote(r_out.at[p], r_in.at[p], r_send.at[k], r_recv.at[p], {"ep": p}).wait_recv()
    ids = ids_ref[...]
    route = jnp.zeros(ids.shape, jnp.float32)
    for p in range(n_ep):
        route = route + jnp.where(ids == p // group, r_in[p, 0:1, :], 0.0)
    rz_out[0:2, :] = route
    rz_out[2:8, :] = jnp.zeros((6, count), jnp.float32)
    for k in range(1, n_et):
        rz_copy(k).start()
    rz_in[i] = rz_out[...]

    for s in range(n_et):
        value = total[s, chip].astype(jnp.float32)
        for k in range(1, chips):
            q = lax.rem(chip + k, chips)
            remote(
                total.at[s, q], x_in.at[s, q], x_send.at[s, k], x_recv.at[s, q],
                {"ep": q * 2 + core},
            ).wait_recv()
            value = value + x_in[s, q].astype(jnp.float32)
        if s < n_et - 1:
            z_out[s] = value.astype(jnp.bfloat16)
            z_copy(s).start()
        else:
            z_in[i] = value.astype(jnp.bfloat16)

    for k in range(1, n_et):
        j = lax.rem(i + k, n_et)
        remote(z_in.at[j], z_in.at[j], z_send.at[0], z_recv.at[j], {"et": j}).wait_recv()
        remote(rz_in.at[j], rz_in.at[j], rz_send.at[k], rz_recv.at[j], {"et": j}).wait_recv()
    result = z_in[0].astype(jnp.float32)
    route = rz_in[0]
    for j in range(1, n_et):
        result = result + z_in[j].astype(jnp.float32)
        route = route + rz_in[j]
    tok_ref[...] = result.astype(jnp.bfloat16)
    rg_ref[...] = route

    for k in range(1, n_ep):
        r_copy(k).wait_send()
    for k in range(1, n_et):
        rz_copy(k).wait_send()
    for s in range(n_et):
        for q in range(chips):
            s_copy(s, q).wait_send()
        for k in range(1, chips):
            x_copy(s, k).wait_send()
        if s < n_et - 1:
            z_copy(s).wait_send()


def dispatch(tokens, out_grad, ids, weight, n_ep, n_et):
    count, width = tokens.shape
    slots = n_ep * CAP
    dma = pltpu.SemaphoreType.DMA
    whole = pl.BlockSpec(memory_space=pltpu.VMEM)
    return pl.pallas_call(
        functools.partial(dispatch_kernel, n_ep, n_et),
        out_shape=(
            jax.ShapeDtypeStruct((slots, n_et * width), jnp.bfloat16),
            jax.ShapeDtypeStruct((slots, n_et * width), jnp.bfloat16),
            jax.ShapeDtypeStruct((slots, n_ep * count), jnp.bfloat16),
            jax.ShapeDtypeStruct((slots, 128), jnp.float32),
        ),
        in_specs=[whole] * 4,
        out_specs=(whole,) * 4,
        scratch_shapes=[
            pltpu.VMEM((2, n_ep, n_et, count, width), jnp.bfloat16),
            pltpu.VMEM((n_ep, 16, count), jnp.float32),
            dma((2, n_ep, n_et)),
            dma((2, 2, n_et)),
            dma((2, n_ep // 2, n_et)),
            dma((2, n_ep, n_et)),
            dma((n_ep,)),
            dma((n_ep,)),
        ],
        compiler_params=pltpu.CompilerParams(
            collective_id=0, has_side_effects=True, vmem_limit_bytes=VMEM_LIMIT
        ),
        name="dispatch",
    )(tokens, out_grad, ids, weight)


def combine(gate_delta, up_delta, w_gate, w_up, place, route, ids, count, n_ep, n_et):
    width = w_gate.shape[0] // n_et
    hidden = w_gate.shape[1]
    chips = n_ep // 2
    dma = pltpu.SemaphoreType.DMA
    whole = pl.BlockSpec(memory_space=pltpu.VMEM)
    hbm = pl.BlockSpec(memory_space=pl.ANY)
    bf16, f32 = jnp.bfloat16, jnp.float32
    return pl.pallas_call(
        functools.partial(combine_kernel, n_ep, n_et),
        out_shape=(
            jax.ShapeDtypeStruct((count, width), bf16),
            jax.ShapeDtypeStruct((8, count), f32),
        ),
        in_specs=[whole, whole, hbm, hbm, whole, whole, whole],
        out_specs=(whole, whole),
        scratch_shapes=[
            pltpu.VMEM((n_et, width, hidden), bf16),
            pltpu.VMEM((n_et, width, hidden), bf16),
            pltpu.VMEM((n_et, n_ep, count, width), bf16),
            pltpu.VMEM((n_et, chips, count, width), bf16),
            pltpu.VMEM((n_et, chips, count, width), bf16),
            pltpu.VMEM((n_et, chips, count, width), bf16),
            pltpu.VMEM((n_et, count, width), bf16),
            pltpu.VMEM((n_et, count, width), bf16),
            pltpu.VMEM((n_ep, 8, count), f32),
            pltpu.VMEM((n_ep, 8, count), f32),
            pltpu.VMEM((8, count), f32),
            pltpu.VMEM((n_et, 8, count), f32),
            dma((2, n_et)),
            dma((n_et, chips)),
            dma((n_et, chips)),
            dma((n_et, chips)),
            dma((n_et, chips)),
            dma((n_et,)),
            dma((n_et,)),
            dma((n_ep,)),
            dma((n_ep,)),
            dma((n_et,)),
            dma((n_et,)),
        ],
        compiler_params=pltpu.CompilerParams(
            collective_id=1, has_side_effects=True, vmem_limit_bytes=VMEM_LIMIT
        ),
        name="combine",
    )(gate_delta, up_delta, w_gate, w_up, place, route, ids)


def body(tokens, out_grad, route_ids, route_weight, w_gate, w_up, w_down):
    n_ep, n_et = lax.axis_size("ep"), lax.axis_size("et")
    count = tokens.shape[0]
    ids = route_ids.T
    flat_x, flat_dy, select, scale_wide = dispatch(
        tokens, out_grad, ids, route_weight.T.astype(jnp.float32), n_ep, n_et
    )
    scale = scale_wide[:, 0:1]
    contract_rows = (((0,), (0,)), ((), ()))
    contract_hidden = (((1,), (1,)), ((), ()))
    gate = jnp.dot(flat_x, w_gate, preferred_element_type=jnp.float32)
    upper = jnp.dot(flat_x, w_up, preferred_element_type=jnp.float32)
    sigma = jax.nn.sigmoid(gate)
    silu_gate = gate * sigma
    active = silu_gate * upper
    scaled = (scale * active).astype(jnp.bfloat16)
    raw_grad = lax.dot_general(flat_dy, w_down, contract_hidden, preferred_element_type=jnp.float32)
    slot_route = jnp.sum(active * raw_grad, axis=1).astype(jnp.bfloat16)
    hidden_grad = scale * raw_grad
    gate_delta = (hidden_grad * upper * sigma * (1.0 + gate * (1.0 - sigma))).astype(jnp.bfloat16)
    up_delta = (hidden_grad * silu_gate).astype(jnp.bfloat16)
    route = jnp.broadcast_to(slot_route[None, :], (16, slot_route.shape[0]))[0:8]
    token_grad, route_rows = combine(
        gate_delta, up_delta, w_gate, w_up, select.T, route, ids, count, n_ep, n_et
    )
    gate_grad = lax.dot_general(
        flat_x, gate_delta, contract_rows, preferred_element_type=jnp.float32
    ).astype(jnp.bfloat16)
    up_grad = lax.dot_general(
        flat_x, up_delta, contract_rows, preferred_element_type=jnp.float32
    ).astype(jnp.bfloat16)
    down_grad = lax.dot_general(
        scaled, flat_dy, contract_rows, preferred_element_type=jnp.float32
    ).astype(jnp.bfloat16)
    return (token_grad, route_rows[0:2].T, gate_grad, up_grad, down_grad)


def solution(mesh):
    return jax.shard_map(
        body,
        mesh=mesh,
        in_specs=(
            P(("rep", "ep"), "et"),
            P(("rep", "ep"), "et"),
            P(("rep", "ep"), None),
            P(("rep", "ep"), None),
            P(None, ("ep", "et")),
            P(None, ("ep", "et")),
            P(("ep", "et"), None),
        ),
        out_specs=(
            P(("rep", "ep"), "et"),
            P(("rep", "ep"), None),
            P("rep", ("ep", "et")),
            P("rep", ("ep", "et")),
            P(("ep", "et"), "rep"),
        ),
        check_vma=False,
    )
```

```python
import functools

import jax
import jax.numpy as jnp
from jax import lax
from jax.experimental import pallas as pl
from jax.experimental.pallas import tpu as pltpu
from jax.sharding import PartitionSpec as P

EXP = 4
CAP = 72
MESH = pl.DeviceIdType.MESH
VMEM_LIMIT = 62 * 1024 * 1024


def remote(src, dst, send_sem, recv_sem, device):
    return pltpu.make_async_remote_copy(
        src_ref=src,
        dst_ref=dst,
        send_sem=send_sem,
        recv_sem=recv_sem,
        device_id=device,
        device_id_type=MESH,
    )


def dispatch_kernel(
    n_ep, n_et, tok_ref, dy_ref, ids_ref, w_ref, wg_ref, wu_ref, wd_ref,
    x_ref, d_ref, gd_ref, ud_ref, scaled_ref, place_ref, route_ref,
    rows, meta, sel, stats, wg, wu, wd, gate, upper,
    recv_sem, z_sem, x_sem, s_sem, meta_send, meta_recv, w_sem,
):
    group = n_ep // EXP
    chips = n_ep // 2
    me, i = lax.axis_index("ep"), lax.axis_index("et")
    chip, core = lax.div(me, 2), lax.rem(me, 2)
    sibling = chip * 2 + 1 - core
    own = (tok_ref, dy_ref)
    width = tok_ref.shape[1]
    count = tok_ref.shape[0]
    hidden = wg.shape[1]
    tile = min(512, hidden)
    weights = [
        pltpu.make_async_copy(source, target, w_sem.at[k])
        for k, (source, target) in enumerate(((wg_ref, wg), (wu_ref, wu), (wd_ref, wd)))
    ]

    barrier = pltpu.get_barrier_semaphore()
    for k in range(1, n_ep):
        pl.semaphore_signal(
            barrier, inc=1, device_id={"ep": lax.rem(me + k, n_ep)}, device_id_type=MESH
        )

    @pl.when(i > 0)
    def _():
        pl.semaphore_signal(barrier, inc=1, device_id={"et": i - 1}, device_id_type=MESH)

    @pl.when(i < n_et - 1)
    def _():
        pl.semaphore_signal(barrier, inc=1, device_id={"et": i + 1}, device_id_type=MESH)

    ids = ids_ref[...]
    weight = w_ref[...]
    experts = lax.broadcasted_iota(jnp.int32, (8, count), 0)
    first, second = ids[0:1, :] == experts, ids[1:2, :] == experts
    hit = jnp.logical_or(first, second)
    earlier = lax.broadcasted_iota(jnp.int32, (count, count), 0) < lax.broadcasted_iota(
        jnp.int32, (count, count), 1
    )
    before = jnp.dot(
        jnp.where(hit, 1.0, 0.0).astype(jnp.bfloat16),
        jnp.where(earlier, 1.0, 0.0).astype(jnp.bfloat16),
        preferred_element_type=jnp.float32,
    )
    meta[me, 0:8, :] = jnp.where(hit, before, -1e6)
    meta[me, 8:16, :] = jnp.where(first, weight[0:1, :], 0.0) + jnp.where(
        second, weight[1:2, :], 0.0
    )

    neighbours = jnp.where(i > 0, 1, 0) + jnp.where(i < n_et - 1, 1, 0)
    pl.semaphore_wait(barrier, n_ep - 1 + neighbours)

    def block(a, p, j):
        return rows.at[a, p, j]

    def z_copy(a, j, way, src):
        return remote(
            src, block(a, me, j), z_sem.at[a, way, j], recv_sem.at[a, me, j],
            {"et": i + 1 if way == 0 else i - 1},
        )

    def x_copy(a, k, j, src):
        peer = lax.rem(chip + k, chips) * 2 + core
        return remote(
            src, block(a, me, j), x_sem.at[a, k, j], recv_sem.at[a, me, j], {"ep": peer}
        )

    def s_copy(a, p, j, src):
        return remote(
            src, block(a, p, j), s_sem.at[a, p, j], recv_sem.at[a, p, j], {"ep": sibling}
        )

    def meta_copy(k):
        return remote(
            meta.at[me], meta.at[me], meta_send.at[k], meta_recv.at[me],
            {"ep": lax.rem(me + k, n_ep)},
        )

    def arrive(a, p, j):
        remote(
            block(a, p, j), block(a, p, j), s_sem.at[a, p, j], recv_sem.at[a, p, j],
            {"ep": sibling},
        ).wait_recv()

    def fan(a, j, src):
        for k in range(1, chips):
            x_copy(a, k, j, src).start()
        s_copy(a, me, j, src).start()

    def send_own(a):
        @pl.when(i < n_et - 1)
        def _():
            z_copy(a, i, 0, own[a]).start()

        @pl.when(i > 0)
        def _():
            z_copy(a, i, 1, own[a]).start()

        fan(a, i, own[a])

    def on_steps(s, act):
        @pl.when(i >= s)
        def _():
            act(i - s, 0)

        if s > 0:
            @pl.when(i + s < n_et)
            def _():
                act(i + s, 1)

    def from_line(a, s):
        def act(j, way):
            arrive(a, me, j)
            if way == 0:
                @pl.when(i < n_et - 1)
                def _():
                    z_copy(a, j, 0, block(a, me, j)).start()
            else:
                @pl.when(i > 0)
                def _():
                    z_copy(a, j, 1, block(a, me, j)).start()

            fan(a, j, block(a, me, j))

        on_steps(s, act)

    def from_chips(a, s):
        def act(j, way):
            for k in range(1, chips):
                p = lax.rem(chip + k, chips) * 2 + core
                arrive(a, p, j)
                s_copy(a, p, j, block(a, p, j)).start()

        on_steps(s, act)

    def pack(a, out):
        for q in range(chips):
            for j in range(n_et):
                arrive(a, q * 2 + 1 - core, j)

        @pl.loop(0, n_et)
        def _(j):
            source = rows[a, :, j].reshape(n_ep * count, width)
            out[:, pl.ds(pl.multiple_of(j * width, width), width)] = jnp.dot(
                sel[...], source, preferred_element_type=jnp.float32
            ).astype(jnp.bfloat16)

    send_own(0)
    for k in range(1, n_ep):
        meta_copy(k).start()
    for copy in weights:
        copy.start()
    for a in range(2):
        rows[a, me, i] = own[a][...]
    for s in range(1, n_et):
        from_line(0, s)
        if s == 1:
            send_own(1)
        from_chips(0, s - 1)
    if n_et == 1:
        send_own(1)

    for k in range(1, n_ep):
        p = lax.rem(me + k, n_ep)
        remote(
            meta.at[p], meta.at[p], meta_send.at[k], meta_recv.at[p], {"ep": p}
        ).wait_recv()
    expert = lax.div(me, group)
    slots = n_ep * CAP
    slot_row = lax.broadcasted_iota(jnp.int32, (slots, count), 0).astype(jnp.float32)
    slot_column = lax.broadcasted_iota(jnp.int32, (count, slots), 1).astype(jnp.float32)
    diagonal = lax.broadcasted_iota(jnp.int32, (count, count), 0) == lax.broadcasted_iota(
        jnp.int32, (count, count), 1
    )
    row_scale = jnp.zeros((slots, 1), jnp.float32)
    for p in range(n_ep):
        at = slice(p * count, (p + 1) * count)
        slot = meta[p, pl.ds(expert, 1), :]
        token_weight = meta[p, pl.ds(expert + 8, 1), :]
        match = slot_row == slot + float(p * CAP)
        sel[:, at] = jnp.where(match, 1.0, 0.0).astype(jnp.bfloat16)
        row_scale = row_scale + jnp.sum(
            jnp.where(match, token_weight, 0.0), axis=1, keepdims=True
        )
        column = jnp.sum(jnp.where(diagonal, slot, 0.0), axis=1, keepdims=True)
        place_ref[at, :] = jnp.where(
            slot_column == column + float(p * CAP), 1.0, 0.0
        ).astype(jnp.bfloat16)
    right = lax.broadcasted_iota(jnp.int32, stats.shape, 1) >= 64
    stats[...] = jnp.where(right, 0.0, row_scale)

    if n_et > 1:
        from_line(1, 1)
    from_chips(0, n_et - 1)
    pack(0, x_ref)
    pending = [functools.partial(from_chips, 1, 0)]
    for s in range(2, n_et):
        pending.append(functools.partial(from_line, 1, s))
        pending.append(functools.partial(from_chips, 1, s - 1))
    if n_et > 1:
        pending.append(functools.partial(from_chips, 1, n_et - 1))
    pending.reverse()
    weights[0].wait()
    weights[1].wait()
    for c in range(hidden // tile):
        at = slice(c * tile, (c + 1) * tile)
        for target, matrix in ((gate, wg), (upper, wu)):
            target[:, at] = jnp.dot(
                x_ref[...], matrix[:, at], preferred_element_type=jnp.float32
            )
            if pending:
                pending.pop()()
    while pending:
        pending.pop()()
    weights[2].wait()
    pack(1, d_ref)

    @pl.loop(0, hidden // tile)
    def _(c):
        start = pl.multiple_of(c * tile, tile)
        at = pl.ds(start, tile)
        raw = lax.dot_general(
            d_ref[...], wd[at, :], (((1,), (1,)), ((), ())), preferred_element_type=jnp.float32
        )
        g, u, weight = gate[:, at], upper[:, at], stats[:, 0:1]
        sigma = jax.nn.sigmoid(g)
        silu = g * sigma
        active = silu * u
        scaled_ref[:, at] = (weight * active).astype(jnp.bfloat16)
        stats[...] += jnp.where(right, jnp.sum(active * raw, axis=1, keepdims=True), 0.0)
        hidden_grad = weight * raw
        gd_ref[:, at] = (hidden_grad * u * sigma * (1.0 + g * (1.0 - sigma))).astype(jnp.bfloat16)
        ud_ref[:, at] = (hidden_grad * silu).astype(jnp.bfloat16)

    slot_route = stats[:, 64:65].astype(jnp.bfloat16).astype(jnp.float32)
    for p in range(n_ep):
        chosen = sel[:, p * count : (p + 1) * count].astype(jnp.float32)
        route_ref[p] = jnp.broadcast_to(
            jnp.sum(chosen * slot_route, axis=0, keepdims=True), (8, count)
        )

    for k in range(1, n_ep):
        meta_copy(k).wait_send()
    for a in range(2):
        for j in range(n_et):
            for k in range(1, chips):
                x_copy(a, k, j, block(a, me, j)).wait_send()
            for q in range(chips):
                p = q * 2 + core
                s_copy(a, p, j, block(a, p, j)).wait_send()

            @pl.when(jnp.logical_and(i < n_et - 1, i >= j))
            def _():
                z_copy(a, j, 0, block(a, me, j)).wait_send()

            @pl.when(jnp.logical_and(i > 0, i <= j))
            def _():
                z_copy(a, j, 1, block(a, me, j)).wait_send()


def combine_kernel(
    n_ep, n_et, gd_ref, ud_ref, wg_ref, wu_ref, place_ref, r_out, ids_ref, tok_ref, rg_ref,
    wg, wu, part, sib_in, total, x_in, z_out, z_in, r_in, rz_out, rz_in,
    w_sem, s_send, s_recv, x_send, x_recv, z_send, z_recv, r_send, r_recv, rz_send, rz_recv,
):
    group = n_ep // EXP
    chips = n_ep // 2
    me, i = lax.axis_index("ep"), lax.axis_index("et")
    chip, core = lax.div(me, 2), lax.rem(me, 2)
    sibling = chip * 2 + 1 - core
    count, width = tok_ref.shape
    barrier = pltpu.get_barrier_semaphore()
    for k in range(1, n_ep):
        pl.semaphore_signal(
            barrier, inc=1, device_id={"ep": lax.rem(me + k, n_ep)}, device_id_type=MESH
        )
    for k in range(1, n_et):
        pl.semaphore_signal(
            barrier, inc=1, device_id={"et": lax.rem(i + k, n_et)}, device_id_type=MESH
        )

    def owner(s):
        return lax.rem(i + 1 + s, n_et)

    def weights(s):
        at = pl.ds(pl.multiple_of(owner(s) * width, width), width)
        return (
            pltpu.make_async_copy(wg_ref.at[at, :], wg.at[s], w_sem.at[0, s]),
            pltpu.make_async_copy(wu_ref.at[at, :], wu.at[s], w_sem.at[1, s]),
        )

    for s in range(n_et):
        for copy in weights(s):
            copy.start()
    transposed = (((1,), (1,)), ((), ()))
    pl.semaphore_wait(barrier, n_ep - 1 + n_et - 1)

    def r_copy(k):
        p = lax.rem(me + k, n_ep)
        return remote(r_out.at[p], r_in.at[me], r_send.at[k], r_recv.at[me], {"ep": p})

    def rz_copy(k):
        return remote(
            rz_out, rz_in.at[i], rz_send.at[k], rz_recv.at[i], {"et": lax.rem(i + k, n_et)}
        )

    def s_copy(s, q):
        return remote(
            part.at[s, q * 2 + 1 - core], sib_in.at[s, q], s_send.at[s, q], s_recv.at[s, q],
            {"ep": sibling},
        )

    def x_copy(s, k):
        q = lax.rem(chip + k, chips)
        return remote(
            total.at[s, q], x_in.at[s, chip], x_send.at[s, k], x_recv.at[s, chip],
            {"ep": q * 2 + core},
        )

    def z_copy(s):
        return remote(
            z_out.at[s], z_in.at[i], z_send.at[s], z_recv.at[i], {"et": owner(s)}
        )

    for k in range(1, n_ep):
        r_copy(k).start()
    r_in[me] = r_out[me]

    def to_chips(s):
        for q in range(chips):
            s_copy(s, q).wait_recv()
            total[s, q] = (
                part[s, q * 2 + core].astype(jnp.float32) + sib_in[s, q].astype(jnp.float32)
            ).astype(jnp.bfloat16)
        for k in range(1, chips):
            x_copy(s, k).start()

    def step(s):
        for copy in weights(s):
            copy.wait()
        piece = lax.dot_general(
            gd_ref[...], wg[s], transposed, preferred_element_type=jnp.float32
        ) + lax.dot_general(ud_ref[...], wu[s], transposed, preferred_element_type=jnp.float32)
        placed = jnp.dot(
            place_ref[...], piece.astype(jnp.bfloat16), preferred_element_type=jnp.float32
        ).astype(jnp.bfloat16)
        part[s] = placed.reshape(n_ep, count, width)
        for q in range(chips):
            s_copy(s, q).start()

    step(0)

    @pl.loop(1, n_et)
    def _(s):
        step(s)
        to_chips(s - 1)

    to_chips(n_et - 1)

    for k in range(1, n_ep):
        p = lax.rem(me + k, n_ep)
        remote(r_out.at[p], r_in.at[p], r_send.at[k], r_recv.at[p], {"ep": p}).wait_recv()
    ids = ids_ref[...]
    route = jnp.zeros(ids.shape, jnp.float32)
    for p in range(n_ep):
        route = route + jnp.where(ids == p // group, r_in[p, 0:1, :], 0.0)
    rz_out[0:2, :] = route
    rz_out[2:8, :] = jnp.zeros((6, count), jnp.float32)
    for k in range(1, n_et):
        rz_copy(k).start()
    rz_in[i] = rz_out[...]

    for s in range(n_et):
        value = total[s, chip].astype(jnp.float32)
        for k in range(1, chips):
            q = lax.rem(chip + k, chips)
            remote(
                total.at[s, q], x_in.at[s, q], x_send.at[s, k], x_recv.at[s, q],
                {"ep": q * 2 + core},
            ).wait_recv()
            value = value + x_in[s, q].astype(jnp.float32)
        if s < n_et - 1:
            z_out[s] = value.astype(jnp.bfloat16)
            z_copy(s).start()
        else:
            z_in[i] = value.astype(jnp.bfloat16)

    for k in range(1, n_et):
        j = lax.rem(i + k, n_et)
        remote(z_in.at[j], z_in.at[j], z_send.at[0], z_recv.at[j], {"et": j}).wait_recv()
        remote(rz_in.at[j], rz_in.at[j], rz_send.at[k], rz_recv.at[j], {"et": j}).wait_recv()
    result = z_in[0].astype(jnp.float32)
    route = rz_in[0]
    for j in range(1, n_et):
        result = result + z_in[j].astype(jnp.float32)
        route = route + rz_in[j]
    tok_ref[...] = result.astype(jnp.bfloat16)
    rg_ref[...] = route

    for k in range(1, n_ep):
        r_copy(k).wait_send()
    for k in range(1, n_et):
        rz_copy(k).wait_send()
    for s in range(n_et):
        for q in range(chips):
            s_copy(s, q).wait_send()
        for k in range(1, chips):
            x_copy(s, k).wait_send()
        if s < n_et - 1:
            z_copy(s).wait_send()


def dispatch(tokens, out_grad, ids, weight, w_gate, w_up, w_down, n_ep, n_et):
    count, width = tokens.shape
    slots = n_ep * CAP
    hidden = w_gate.shape[1]
    dma = pltpu.SemaphoreType.DMA
    bf16, f32 = jnp.bfloat16, jnp.float32
    whole = pl.BlockSpec(memory_space=pltpu.VMEM)
    hbm = pl.BlockSpec(memory_space=pl.ANY)
    return pl.pallas_call(
        functools.partial(dispatch_kernel, n_ep, n_et),
        out_shape=(
            jax.ShapeDtypeStruct((slots, n_et * width), bf16),
            jax.ShapeDtypeStruct((slots, n_et * width), bf16),
            jax.ShapeDtypeStruct((slots, hidden), bf16),
            jax.ShapeDtypeStruct((slots, hidden), bf16),
            jax.ShapeDtypeStruct((slots, hidden), bf16),
            jax.ShapeDtypeStruct((n_ep * count, slots), bf16),
            jax.ShapeDtypeStruct((n_ep, 8, count), f32),
        ),
        in_specs=[whole] * 4 + [hbm] * 3,
        out_specs=(whole,) * 7,
        scratch_shapes=[
            pltpu.VMEM((2, n_ep, n_et, count, width), bf16),
            pltpu.VMEM((n_ep, 16, count), f32),
            pltpu.VMEM((slots, n_ep * count), bf16),
            pltpu.VMEM((slots, 128), f32),
            pltpu.VMEM(w_gate.shape, bf16),
            pltpu.VMEM(w_up.shape, bf16),
            pltpu.VMEM(w_down.shape, bf16),
            pltpu.VMEM((slots, hidden), f32),
            pltpu.VMEM((slots, hidden), f32),
            dma((2, n_ep, n_et)),
            dma((2, 2, n_et)),
            dma((2, n_ep // 2, n_et)),
            dma((2, n_ep, n_et)),
            dma((n_ep,)),
            dma((n_ep,)),
            dma((3,)),
        ],
        compiler_params=pltpu.CompilerParams(
            collective_id=0, has_side_effects=True, vmem_limit_bytes=VMEM_LIMIT
        ),
        name="dispatch",
    )(tokens, out_grad, ids, weight, w_gate, w_up, w_down)


def combine(gate_delta, up_delta, w_gate, w_up, place, route, ids, count, n_ep, n_et):
    width = w_gate.shape[0] // n_et
    hidden = w_gate.shape[1]
    chips = n_ep // 2
    dma = pltpu.SemaphoreType.DMA
    whole = pl.BlockSpec(memory_space=pltpu.VMEM)
    hbm = pl.BlockSpec(memory_space=pl.ANY)
    bf16, f32 = jnp.bfloat16, jnp.float32
    return pl.pallas_call(
        functools.partial(combine_kernel, n_ep, n_et),
        out_shape=(
            jax.ShapeDtypeStruct((count, width), bf16),
            jax.ShapeDtypeStruct((8, count), f32),
        ),
        in_specs=[whole, whole, hbm, hbm, whole, whole, whole],
        out_specs=(whole, whole),
        scratch_shapes=[
            pltpu.VMEM((n_et, width, hidden), bf16),
            pltpu.VMEM((n_et, width, hidden), bf16),
            pltpu.VMEM((n_et, n_ep, count, width), bf16),
            pltpu.VMEM((n_et, chips, count, width), bf16),
            pltpu.VMEM((n_et, chips, count, width), bf16),
            pltpu.VMEM((n_et, chips, count, width), bf16),
            pltpu.VMEM((n_et, count, width), bf16),
            pltpu.VMEM((n_et, count, width), bf16),
            pltpu.VMEM((n_ep, 8, count), f32),
            pltpu.VMEM((8, count), f32),
            pltpu.VMEM((n_et, 8, count), f32),
            dma((2, n_et)),
            dma((n_et, chips)),
            dma((n_et, chips)),
            dma((n_et, chips)),
            dma((n_et, chips)),
            dma((n_et,)),
            dma((n_et,)),
            dma((n_ep,)),
            dma((n_ep,)),
            dma((n_et,)),
            dma((n_et,)),
        ],
        compiler_params=pltpu.CompilerParams(
            collective_id=1, has_side_effects=True, vmem_limit_bytes=VMEM_LIMIT
        ),
        name="combine",
    )(gate_delta, up_delta, w_gate, w_up, place, route, ids)


def body(tokens, out_grad, route_ids, route_weight, w_gate, w_up, w_down):
    n_ep, n_et = lax.axis_size("ep"), lax.axis_size("et")
    count = tokens.shape[0]
    ids = route_ids.T
    flat_x, flat_dy, gate_delta, up_delta, scaled, place, route = dispatch(
        tokens, out_grad, ids, route_weight.T.astype(jnp.float32), w_gate, w_up, w_down, n_ep, n_et
    )
    token_grad, route_rows = combine(
        gate_delta, up_delta, w_gate, w_up, place, route, ids, count, n_ep, n_et
    )
    contract_rows = (((0,), (0,)), ((), ()))
    gate_grad = lax.dot_general(
        flat_x, gate_delta, contract_rows, preferred_element_type=jnp.float32
    ).astype(jnp.bfloat16)
    up_grad = lax.dot_general(
        flat_x, up_delta, contract_rows, preferred_element_type=jnp.float32
    ).astype(jnp.bfloat16)
    down_grad = lax.dot_general(
        scaled, flat_dy, contract_rows, preferred_element_type=jnp.float32
    ).astype(jnp.bfloat16)
    return (token_grad, route_rows[0:2].T, gate_grad, up_grad, down_grad)


def solution(mesh):
    return jax.shard_map(
        body,
        mesh=mesh,
        in_specs=(
            P(("rep", "ep"), "et"),
            P(("rep", "ep"), "et"),
            P(("rep", "ep"), None),
            P(("rep", "ep"), None),
            P(None, ("ep", "et")),
            P(None, ("ep", "et")),
            P(("ep", "et"), None),
        ),
        out_specs=(
            P(("rep", "ep"), "et"),
            P(("rep", "ep"), None),
            P("rep", ("ep", "et")),
            P("rep", ("ep", "et")),
            P(("ep", "et"), "rep"),
        ),
        check_vma=False,
    )
```

```python
import functools

import jax
import jax.numpy as jnp
from jax import lax
from jax.experimental import pallas as pl
from jax.experimental.pallas import tpu as pltpu
from jax.sharding import PartitionSpec as P

EXP = 4
CAP = 72
MESH = pl.DeviceIdType.MESH
VMEM_LIMIT = 62 * 1024 * 1024


def remote(src, dst, send_sem, recv_sem, device):
    return pltpu.make_async_remote_copy(
        src_ref=src,
        dst_ref=dst,
        send_sem=send_sem,
        recv_sem=recv_sem,
        device_id=device,
        device_id_type=MESH,
    )


def dispatch_kernel(
    n_ep, n_et, tok_ref, dy_ref, ids_ref, w_ref, wg_ref, wu_ref, wd_ref,
    x_ref, d_ref, gd_ref, ud_ref, scaled_ref, place_ref, route_ref,
    rows, meta, sel, stats, wg, wu, wd, gate, upper,
    recv_sem, z_sem, x_sem, s_sem, meta_send, meta_recv, w_sem,
):
    group = n_ep // EXP
    chips = n_ep // 2
    me, i = lax.axis_index("ep"), lax.axis_index("et")
    chip, core = lax.div(me, 2), lax.rem(me, 2)
    sibling = chip * 2 + 1 - core
    own = (tok_ref, dy_ref)
    width = tok_ref.shape[1]
    count = tok_ref.shape[0]
    hidden = wg.shape[1]
    tile = min(512, hidden)
    weights = [
        pltpu.make_async_copy(source, target, w_sem.at[k])
        for k, (source, target) in enumerate(((wg_ref, wg), (wu_ref, wu), (wd_ref, wd)))
    ]

    barrier = pltpu.get_barrier_semaphore()
    for k in range(1, n_ep):
        pl.semaphore_signal(
            barrier, inc=1, device_id={"ep": lax.rem(me + k, n_ep)}, device_id_type=MESH
        )

    @pl.when(i > 0)
    def _():
        pl.semaphore_signal(barrier, inc=1, device_id={"et": i - 1}, device_id_type=MESH)

    @pl.when(i < n_et - 1)
    def _():
        pl.semaphore_signal(barrier, inc=1, device_id={"et": i + 1}, device_id_type=MESH)

    ids = ids_ref[...]
    weight = w_ref[...]
    experts = lax.broadcasted_iota(jnp.int32, (8, count), 0)
    first, second = ids[0:1, :] == experts, ids[1:2, :] == experts
    hit = jnp.logical_or(first, second)
    earlier = lax.broadcasted_iota(jnp.int32, (count, count), 0) < lax.broadcasted_iota(
        jnp.int32, (count, count), 1
    )
    before = jnp.dot(
        jnp.where(hit, 1.0, 0.0).astype(jnp.bfloat16),
        jnp.where(earlier, 1.0, 0.0).astype(jnp.bfloat16),
        preferred_element_type=jnp.float32,
    )
    meta[me, 0:8, :] = jnp.where(hit, before, -1e6)
    meta[me, 8:16, :] = jnp.where(first, weight[0:1, :], 0.0) + jnp.where(
        second, weight[1:2, :], 0.0
    )

    neighbours = jnp.where(i > 0, 1, 0) + jnp.where(i < n_et - 1, 1, 0)
    pl.semaphore_wait(barrier, n_ep - 1 + neighbours)

    def block(a, p, j):
        return rows.at[a, p, j]

    def z_copy(a, j, way, src):
        return remote(
            src, block(a, me, j), z_sem.at[a, way, j], recv_sem.at[a, me, j],
            {"et": i + 1 if way == 0 else i - 1},
        )

    def x_copy(a, k, j, src):
        peer = lax.rem(chip + k, chips) * 2 + core
        return remote(
            src, block(a, me, j), x_sem.at[a, k, j], recv_sem.at[a, me, j], {"ep": peer}
        )

    def s_copy(a, p, j, src):
        return remote(
            src, block(a, p, j), s_sem.at[a, p, j], recv_sem.at[a, p, j], {"ep": sibling}
        )

    def meta_copy(k):
        return remote(
            meta.at[me], meta.at[me], meta_send.at[k], meta_recv.at[me],
            {"ep": lax.rem(me + k, n_ep)},
        )

    def arrive(a, p, j):
        remote(
            block(a, p, j), block(a, p, j), s_sem.at[a, p, j], recv_sem.at[a, p, j],
            {"ep": sibling},
        ).wait_recv()

    def fan(a, j, src):
        for k in range(1, chips):
            x_copy(a, k, j, src).start()
        s_copy(a, me, j, src).start()

    def send_own(a):
        @pl.when(i < n_et - 1)
        def _():
            z_copy(a, i, 0, own[a]).start()

        @pl.when(i > 0)
        def _():
            z_copy(a, i, 1, own[a]).start()

        fan(a, i, own[a])

    def on_steps(s, act):
        @pl.when(i >= s)
        def _():
            act(i - s, 0)

        if s > 0:
            @pl.when(i + s < n_et)
            def _():
                act(i + s, 1)

    def from_line(a, s):
        def act(j, way):
            arrive(a, me, j)
            if way == 0:
                @pl.when(i < n_et - 1)
                def _():
                    z_copy(a, j, 0, block(a, me, j)).start()
            else:
                @pl.when(i > 0)
                def _():
                    z_copy(a, j, 1, block(a, me, j)).start()

            fan(a, j, block(a, me, j))

        on_steps(s, act)

    def from_chips(a, s):
        def act(j, way):
            for k in range(1, chips):
                p = lax.rem(chip + k, chips) * 2 + core
                arrive(a, p, j)
                s_copy(a, p, j, block(a, p, j)).start()

        on_steps(s, act)

    def pack(a, out):
        for q in range(chips):
            for j in range(n_et):
                arrive(a, q * 2 + 1 - core, j)

        @pl.loop(0, n_et)
        def _(j):
            source = rows[a, :, j].reshape(n_ep * count, width)
            out[:, pl.ds(pl.multiple_of(j * width, width), width)] = jnp.dot(
                sel[...], source, preferred_element_type=jnp.float32
            ).astype(jnp.bfloat16)

    send_own(0)
    for k in range(1, n_ep):
        meta_copy(k).start()
    for copy in weights:
        copy.start()
    for a in range(2):
        rows[a, me, i] = own[a][...]
    for s in range(1, n_et):
        from_line(0, s)
        if s == 1:
            send_own(1)
        from_chips(0, s - 1)
    if n_et == 1:
        send_own(1)

    for k in range(1, n_ep):
        p = lax.rem(me + k, n_ep)
        remote(
            meta.at[p], meta.at[p], meta_send.at[k], meta_recv.at[p], {"ep": p}
        ).wait_recv()
    expert = lax.div(me, group)
    slots = n_ep * CAP
    slot_row = lax.broadcasted_iota(jnp.int32, (slots, count), 0).astype(jnp.float32)
    slot_column = lax.broadcasted_iota(jnp.int32, (count, slots), 1).astype(jnp.float32)
    diagonal = lax.broadcasted_iota(jnp.int32, (count, count), 0) == lax.broadcasted_iota(
        jnp.int32, (count, count), 1
    )
    row_scale = jnp.zeros((slots, 1), jnp.float32)
    for p in range(n_ep):
        at = slice(p * count, (p + 1) * count)
        slot = meta[p, pl.ds(expert, 1), :]
        token_weight = meta[p, pl.ds(expert + 8, 1), :]
        match = slot_row == slot + float(p * CAP)
        sel[:, at] = jnp.where(match, 1.0, 0.0).astype(jnp.bfloat16)
        row_scale = row_scale + jnp.sum(
            jnp.where(match, token_weight, 0.0), axis=1, keepdims=True
        )
        column = jnp.sum(jnp.where(diagonal, slot, 0.0), axis=1, keepdims=True)
        place_ref[at, :] = jnp.where(
            slot_column == column + float(p * CAP), 1.0, 0.0
        ).astype(jnp.bfloat16)
    right = lax.broadcasted_iota(jnp.int32, stats.shape, 1) >= 64
    stats[...] = jnp.where(right, 0.0, row_scale)

    if n_et > 1:
        from_line(1, 1)
    from_chips(0, n_et - 1)
    pack(0, x_ref)
    pending = [functools.partial(from_chips, 1, 0)]
    for s in range(2, n_et):
        pending.append(functools.partial(from_line, 1, s))
        pending.append(functools.partial(from_chips, 1, s - 1))
    if n_et > 1:
        pending.append(functools.partial(from_chips, 1, n_et - 1))
    pending.reverse()
    weights[0].wait()
    weights[1].wait()
    for c in range(hidden // tile):
        at = slice(c * tile, (c + 1) * tile)
        for target, matrix in ((gate, wg), (upper, wu)):
            target[:, at] = jnp.dot(
                x_ref[...], matrix[:, at], preferred_element_type=jnp.float32
            )
            if pending:
                pending.pop()()
    while pending:
        pending.pop()()
    weights[2].wait()
    pack(1, d_ref)

    @pl.loop(0, hidden // tile)
    def _(c):
        start = pl.multiple_of(c * tile, tile)
        at = pl.ds(start, tile)
        raw = lax.dot_general(
            d_ref[...], wd[at, :], (((1,), (1,)), ((), ())), preferred_element_type=jnp.float32
        )
        g, u, weight = gate[:, at], upper[:, at], stats[:, 0:1]
        sigma = jax.nn.sigmoid(g)
        silu = g * sigma
        active = silu * u
        scaled_ref[:, at] = (weight * active).astype(jnp.bfloat16)
        stats[...] += jnp.where(right, jnp.sum(active * raw, axis=1, keepdims=True), 0.0)
        hidden_grad = weight * raw
        gd_ref[:, at] = (hidden_grad * u * sigma * (1.0 + g * (1.0 - sigma))).astype(jnp.bfloat16)
        ud_ref[:, at] = (hidden_grad * silu).astype(jnp.bfloat16)

    slot_route = stats[:, 64:65].astype(jnp.bfloat16).astype(jnp.float32)
    for p in range(n_ep):
        chosen = sel[:, p * count : (p + 1) * count].astype(jnp.float32)
        route_ref[p] = jnp.broadcast_to(
            jnp.sum(chosen * slot_route, axis=0, keepdims=True), (8, count)
        )

    for k in range(1, n_ep):
        meta_copy(k).wait_send()
    for a in range(2):
        for j in range(n_et):
            for k in range(1, chips):
                x_copy(a, k, j, block(a, me, j)).wait_send()
            for q in range(chips):
                p = q * 2 + core
                s_copy(a, p, j, block(a, p, j)).wait_send()

            @pl.when(jnp.logical_and(i < n_et - 1, i >= j))
            def _():
                z_copy(a, j, 0, block(a, me, j)).wait_send()

            @pl.when(jnp.logical_and(i > 0, i <= j))
            def _():
                z_copy(a, j, 1, block(a, me, j)).wait_send()


def combine_kernel(
    n_ep, n_et, gd_ref, ud_ref, wg_ref, wu_ref, place_ref, r_out, ids_ref, tok_ref, rg_ref,
    wg, wu, part, sib_in, total, x_in, z_out, z_in, r_in, rz_out, rz_in,
    w_sem, s_send, s_recv, x_send, x_recv, z_send, z_recv, r_send, r_recv, rz_send, rz_recv,
):
    group = n_ep // EXP
    chips = n_ep // 2
    me, i = lax.axis_index("ep"), lax.axis_index("et")
    chip, core = lax.div(me, 2), lax.rem(me, 2)
    sibling = chip * 2 + 1 - core
    count, width = tok_ref.shape
    sub = wg.shape[1]
    pieces = width // sub
    steps = n_et * pieces
    barrier = pltpu.get_barrier_semaphore()
    for k in range(1, n_ep):
        pl.semaphore_signal(
            barrier, inc=1, device_id={"ep": lax.rem(me + k, n_ep)}, device_id_type=MESH
        )
    for k in range(1, n_et):
        pl.semaphore_signal(
            barrier, inc=1, device_id={"et": lax.rem(i + k, n_et)}, device_id_type=MESH
        )

    def owner(s):
        return lax.rem(i + 1 + lax.div(s, pieces), n_et)

    def weights(s):
        first = owner(s) * width + lax.rem(s, pieces) * sub
        at = pl.ds(pl.multiple_of(first, sub), sub)
        return (
            pltpu.make_async_copy(wg_ref.at[at, :], wg.at[s], w_sem.at[0, s]),
            pltpu.make_async_copy(wu_ref.at[at, :], wu.at[s], w_sem.at[1, s]),
        )

    @pl.loop(0, steps)
    def _(s):
        for copy in weights(s):
            copy.start()

    transposed = (((1,), (1,)), ((), ()))
    pl.semaphore_wait(barrier, n_ep - 1 + n_et - 1)

    def r_copy(k):
        p = lax.rem(me + k, n_ep)
        return remote(r_out.at[p], r_in.at[me], r_send.at[k], r_recv.at[me], {"ep": p})

    def rz_copy(k):
        return remote(
            rz_out, rz_in.at[i], rz_send.at[k], rz_recv.at[i], {"et": lax.rem(i + k, n_et)}
        )

    def s_copy(s, q):
        return remote(
            part.at[s, q * 2 + 1 - core], sib_in.at[s, q], s_send.at[s, q], s_recv.at[s, q],
            {"ep": sibling},
        )

    def x_copy(s, k):
        q = lax.rem(chip + k, chips)
        return remote(
            total.at[s, q], x_in.at[s, chip], x_send.at[s, k], x_recv.at[s, chip],
            {"ep": q * 2 + core},
        )

    def z_copy(s):
        return remote(
            z_out.at[s], z_in.at[i, lax.rem(s, pieces)], z_send.at[s],
            z_recv.at[i, lax.rem(s, pieces)], {"et": owner(s)},
        )

    for k in range(1, n_ep):
        r_copy(k).start()
    r_in[me] = r_out[me]

    def to_chips(s):
        for q in range(chips):
            s_copy(s, q).wait_recv()
            total[s, q] = (
                part[s, q * 2 + core].astype(jnp.float32) + sib_in[s, q].astype(jnp.float32)
            ).astype(jnp.bfloat16)
        for k in range(1, chips):
            x_copy(s, k).start()

    def step(s):
        for copy in weights(s):
            copy.wait()
        piece = lax.dot_general(
            gd_ref[...], wg[s], transposed, preferred_element_type=jnp.float32
        ) + lax.dot_general(ud_ref[...], wu[s], transposed, preferred_element_type=jnp.float32)
        placed = jnp.dot(
            place_ref[...], piece.astype(jnp.bfloat16), preferred_element_type=jnp.float32
        ).astype(jnp.bfloat16)
        part[s] = placed.reshape(n_ep, count, sub)
        for q in range(chips):
            s_copy(s, q).start()

    step(0)

    @pl.loop(1, steps)
    def _(s):
        step(s)
        to_chips(s - 1)

    to_chips(steps - 1)

    for k in range(1, n_ep):
        p = lax.rem(me + k, n_ep)
        remote(r_out.at[p], r_in.at[p], r_send.at[k], r_recv.at[p], {"ep": p}).wait_recv()
    ids = ids_ref[...]
    route = jnp.zeros(ids.shape, jnp.float32)
    for p in range(n_ep):
        route = route + jnp.where(ids == p // group, r_in[p, 0:1, :], 0.0)
    rz_out[0:2, :] = route
    rz_out[2:8, :] = jnp.zeros((6, count), jnp.float32)
    for k in range(1, n_et):
        rz_copy(k).start()
    rz_in[i] = rz_out[...]

    def gather_chips(s):
        value = total[s, chip].astype(jnp.float32)
        for k in range(1, chips):
            q = lax.rem(chip + k, chips)
            remote(
                total.at[s, q], x_in.at[s, q], x_send.at[s, k], x_recv.at[s, q],
                {"ep": q * 2 + core},
            ).wait_recv()
            value = value + x_in[s, q].astype(jnp.float32)
        return value.astype(jnp.bfloat16)

    @pl.loop(0, steps - pieces)
    def _(s):
        z_out[s] = gather_chips(s)
        z_copy(s).start()

    for u in range(pieces):
        z_in[i, u] = gather_chips(steps - pieces + u)

    for k in range(1, n_et):
        j = lax.rem(i + k, n_et)
        for u in range(pieces):
            remote(
                z_in.at[j, u], z_in.at[j, u], z_send.at[0], z_recv.at[j, u], {"et": j}
            ).wait_recv()
        remote(rz_in.at[j], rz_in.at[j], rz_send.at[k], rz_recv.at[j], {"et": j}).wait_recv()
    route = rz_in[0]
    for j in range(1, n_et):
        route = route + rz_in[j]
    for u in range(pieces):
        result = z_in[0, u].astype(jnp.float32)
        for j in range(1, n_et):
            result = result + z_in[j, u].astype(jnp.float32)
        tok_ref[:, u * sub : (u + 1) * sub] = result.astype(jnp.bfloat16)
    rg_ref[...] = route

    for k in range(1, n_ep):
        r_copy(k).wait_send()
    for k in range(1, n_et):
        rz_copy(k).wait_send()

    @pl.loop(0, steps)
    def _(s):
        for q in range(chips):
            s_copy(s, q).wait_send()
        for k in range(1, chips):
            x_copy(s, k).wait_send()

    @pl.loop(0, steps - pieces)
    def _(s):
        z_copy(s).wait_send()


def dispatch(tokens, out_grad, ids, weight, w_gate, w_up, w_down, n_ep, n_et):
    count, width = tokens.shape
    slots = n_ep * CAP
    hidden = w_gate.shape[1]
    dma = pltpu.SemaphoreType.DMA
    bf16, f32 = jnp.bfloat16, jnp.float32
    whole = pl.BlockSpec(memory_space=pltpu.VMEM)
    hbm = pl.BlockSpec(memory_space=pl.ANY)
    return pl.pallas_call(
        functools.partial(dispatch_kernel, n_ep, n_et),
        out_shape=(
            jax.ShapeDtypeStruct((slots, n_et * width), bf16),
            jax.ShapeDtypeStruct((slots, n_et * width), bf16),
            jax.ShapeDtypeStruct((slots, hidden), bf16),
            jax.ShapeDtypeStruct((slots, hidden), bf16),
            jax.ShapeDtypeStruct((slots, hidden), bf16),
            jax.ShapeDtypeStruct((n_ep * count, slots), bf16),
            jax.ShapeDtypeStruct((n_ep, 8, count), f32),
        ),
        in_specs=[whole] * 4 + [hbm] * 3,
        out_specs=(whole,) * 7,
        scratch_shapes=[
            pltpu.VMEM((2, n_ep, n_et, count, width), bf16),
            pltpu.VMEM((n_ep, 16, count), f32),
            pltpu.VMEM((slots, n_ep * count), bf16),
            pltpu.VMEM((slots, 128), f32),
            pltpu.VMEM(w_gate.shape, bf16),
            pltpu.VMEM(w_up.shape, bf16),
            pltpu.VMEM(w_down.shape, bf16),
            pltpu.VMEM((slots, hidden), f32),
            pltpu.VMEM((slots, hidden), f32),
            dma((2, n_ep, n_et)),
            dma((2, 2, n_et)),
            dma((2, n_ep // 2, n_et)),
            dma((2, n_ep, n_et)),
            dma((n_ep,)),
            dma((n_ep,)),
            dma((3,)),
        ],
        compiler_params=pltpu.CompilerParams(
            collective_id=0, has_side_effects=True, vmem_limit_bytes=VMEM_LIMIT
        ),
        name="dispatch",
    )(tokens, out_grad, ids, weight, w_gate, w_up, w_down)


def combine(gate_delta, up_delta, w_gate, w_up, place, route, ids, count, n_ep, n_et):
    width = w_gate.shape[0] // n_et
    hidden = w_gate.shape[1]
    chips = n_ep // 2
    sub = 256 if width % 256 == 0 else 128
    pieces = width // sub
    steps = n_et * pieces
    dma = pltpu.SemaphoreType.DMA
    whole = pl.BlockSpec(memory_space=pltpu.VMEM)
    hbm = pl.BlockSpec(memory_space=pl.ANY)
    bf16, f32 = jnp.bfloat16, jnp.float32
    return pl.pallas_call(
        functools.partial(combine_kernel, n_ep, n_et),
        out_shape=(
            jax.ShapeDtypeStruct((count, width), bf16),
            jax.ShapeDtypeStruct((8, count), f32),
        ),
        in_specs=[whole, whole, hbm, hbm, whole, whole, whole],
        out_specs=(whole, whole),
        scratch_shapes=[
            pltpu.VMEM((steps, sub, hidden), bf16),
            pltpu.VMEM((steps, sub, hidden), bf16),
            pltpu.VMEM((steps, n_ep, count, sub), bf16),
            pltpu.VMEM((steps, chips, count, sub), bf16),
            pltpu.VMEM((steps, chips, count, sub), bf16),
            pltpu.VMEM((steps, chips, count, sub), bf16),
            pltpu.VMEM((steps, count, sub), bf16),
            pltpu.VMEM((n_et, pieces, count, sub), bf16),
            pltpu.VMEM((n_ep, 8, count), f32),
            pltpu.VMEM((8, count), f32),
            pltpu.VMEM((n_et, 8, count), f32),
            dma((2, steps)),
            dma((steps, chips)),
            dma((steps, chips)),
            dma((steps, chips)),
            dma((steps, chips)),
            dma((steps,)),
            dma((n_et, pieces)),
            dma((n_ep,)),
            dma((n_ep,)),
            dma((n_et,)),
            dma((n_et,)),
        ],
        compiler_params=pltpu.CompilerParams(
            collective_id=1, has_side_effects=True, vmem_limit_bytes=VMEM_LIMIT
        ),
        name="combine",
    )(gate_delta, up_delta, w_gate, w_up, place, route, ids)


def grads_kernel(x_ref, gd_ref, ud_ref, scaled_ref, d_ref, gate_ref, up_ref, down_ref):
    contract_rows = (((0,), (0,)), ((), ()))
    for left, right, out in (
        (x_ref, gd_ref, gate_ref), (x_ref, ud_ref, up_ref), (scaled_ref, d_ref, down_ref)
    ):
        out[...] = lax.dot_general(
            left[...], right[...], contract_rows, preferred_element_type=jnp.float32
        ).astype(jnp.bfloat16)


def weight_grads(x, gate_delta, up_delta, scaled, dy):
    slots, width = x.shape
    hidden = gate_delta.shape[1]
    steps = max(1, hidden // 256)
    rows, hidden_rows = width // steps, hidden // steps

    def full(columns):
        return pl.BlockSpec((slots, columns), lambda t: (0, 0))

    def columns_of(size):
        return pl.BlockSpec((slots, size), lambda t: (0, t))

    def rows_of(size, columns):
        return pl.BlockSpec((size, columns), lambda t: (t, 0))

    return pl.pallas_call(
        grads_kernel,
        grid=(steps,),
        in_specs=[columns_of(rows), full(hidden), full(hidden), columns_of(hidden_rows), full(width)],
        out_specs=(rows_of(rows, hidden), rows_of(rows, hidden), rows_of(hidden_rows, width)),
        out_shape=(
            jax.ShapeDtypeStruct((width, hidden), jnp.bfloat16),
            jax.ShapeDtypeStruct((width, hidden), jnp.bfloat16),
            jax.ShapeDtypeStruct((hidden, width), jnp.bfloat16),
        ),
        compiler_params=pltpu.CompilerParams(vmem_limit_bytes=VMEM_LIMIT),
        name="weight_grads",
    )(x, gate_delta, up_delta, scaled, dy)


def body(tokens, out_grad, route_ids, route_weight, w_gate, w_up, w_down):
    n_ep, n_et = lax.axis_size("ep"), lax.axis_size("et")
    count = tokens.shape[0]
    ids = route_ids.T
    flat_x, flat_dy, gate_delta, up_delta, scaled, place, route = dispatch(
        tokens, out_grad, ids, route_weight.T.astype(jnp.float32), w_gate, w_up, w_down, n_ep, n_et
    )
    token_grad, route_rows = combine(
        gate_delta, up_delta, w_gate, w_up, place, route, ids, count, n_ep, n_et
    )
    gate_grad, up_grad, down_grad = weight_grads(flat_x, gate_delta, up_delta, scaled, flat_dy)
    return (token_grad, route_rows[0:2].T, gate_grad, up_grad, down_grad)


def solution(mesh):
    return jax.shard_map(
        body,
        mesh=mesh,
        in_specs=(
            P(("rep", "ep"), "et"),
            P(("rep", "ep"), "et"),
            P(("rep", "ep"), None),
            P(("rep", "ep"), None),
            P(None, ("ep", "et")),
            P(None, ("ep", "et")),
            P(("ep", "et"), None),
        ),
        out_specs=(
            P(("rep", "ep"), "et"),
            P(("rep", "ep"), None),
            P("rep", ("ep", "et")),
            P("rep", ("ep", "et")),
            P(("ep", "et"), "rep"),
        ),
        check_vma=False,
    )
```
